128 devices in a mesh: outer: 4 (over z_lo, core), fsdp: 32 (over y, z_hi, x).
Axes of the slice: x: 4, y: 4, z: 4 (z_hi: 2, z_lo: 2; z = z_hi * 2 + z_lo), core: 2. Of those that a mesh axis runs over, the one named last changes fastest.
Arguments:
- partials: bfloat16 [128, 32768, 128], P(('outer', 'fsdp')), may hold values from -4 to 4
- worker_residual: float32 [4, 32768, 128], P('outer', 'fsdp'), may hold values from -4 to 4
- server_residual: float32 [32, 1024, 128], P('fsdp', 'outer'), may hold values from -4 to 4
- master: float32 [32, 1024, 128], P('fsdp', 'outer'), may hold values from -0.3 to 0.3
- first_moment: float32 [32, 1024, 128], P('fsdp', 'outer'), may hold values from -6 to 6
- second_moment: float32 [32, 1024, 128], P('fsdp', 'outer'), may hold values from 0.5 to 50
Outputs:
- new_master: float32 [32, 1024, 128], P('fsdp', 'outer')
- new_first: float32 [32, 1024, 128], P('fsdp', 'outer')
- new_second: float32 [32, 1024, 128], P('fsdp', 'outer')
- params_full: bfloat16 [32768, 128], replicated
The draws below stay inside these ranges and needn't reach their ends.
All inputs are finite; a program needn't handle non-finite values. Where the reference program divides by a largest or mean magnitude, that divisor is 1e-20 or more.
Results may differ from the reference program's by a relative error of at most 0.0035.
Values may be sent and summed in bfloat16 or wider, within the bound.
A program may use at most 128 MiB of HBM per device.

```python
import math
import jax
import jax.numpy as jnp
from jax import lax

BLOCK = 128
STEP = 10
BLOCKS = 32768
PODS = 4
SHARDS = 32
REPLICAS = 128
P_BLK = 1024


def spiked(drawn, stream_key, source, target, blocks, factor):
    def block_of(axis_at):
        return (jnp.arange(drawn.shape[axis_at]) // (drawn.shape[axis_at] // blocks)).reshape((-1,) + (1,) * (drawn.ndim - 1 - axis_at))

    one_side = jax.random.permutation(stream_key, blocks)[block_of(target)]
    other_side = (block_of(target) + blocks // 2) % blocks
    return jnp.where((block_of(source) == one_side) | (block_of(source) == other_side), factor * drawn, drawn)


def block_levels(key, shape, cuts, least, largest):
    factor_of = 1.0
    for dim, parts in cuts:
        heights = jax.random.uniform(jax.random.fold_in(jax.random.fold_in(key, 6), dim), (parts,), jnp.float32, least / len(cuts), largest / len(cuts))
        factor_of = factor_of * jnp.repeat(jnp.exp(heights), shape[dim] // parts).reshape((-1,) + (1,) * (len(shape) - 1 - dim))
    return factor_of


def noise(rng, extent, deviation, bound, pieces=(), dtype=jnp.bfloat16):
    gain = block_levels(rng, extent, pieces, -0.22, 0.18) if pieces else 1.0
    values = jax.random.normal(rng, extent, jnp.float32) * deviation * gain
    return jnp.minimum(jnp.maximum(values, -bound), bound).astype(dtype)


def gaussian_with(key, shape, scale, most, split, heavy, held_as=jnp.bfloat16):
    array = scale * jax.random.normal(key, shape, jnp.float32)
    if split:
        array = array * block_levels(key, shape, split, -0.22, 0.18)
    return jnp.clip(spiked(array, jax.random.fold_in(key, 3), *heavy), -most, most).astype(held_as)


def setup_inputs(seed: int = 0) -> dict:
    keys = jax.random.split(jax.random.key(seed), 7)
    partials = gaussian_with(keys[0], (REPLICAS, BLOCKS, BLOCK), (SHARDS ** -0.5), 4.0, ((0, 128),), (0, 1, 128, 5.5))
    worker_residual = noise(keys[1], (PODS, BLOCKS, BLOCK), 0.5, 4.0, ((0, 4), (1, 32)), jnp.float32)
    server_residual = noise(keys[2], (SHARDS, P_BLK, BLOCK), 0.5, 4.0, ((0, 32), (1, 4)), jnp.float32)
    master = noise(keys[3], (SHARDS, P_BLK, BLOCK), 0.05, 0.3, ((0, 32), (1, 4)), jnp.float32)
    first_moment = noise(keys[4], (SHARDS, P_BLK, BLOCK), 1.0, 6.0, ((0, 32), (1, 4)), jnp.float32)
    second_moment = jnp.clip(jnp.exp(math.log(50.0) - 4.6051702 * jax.random.uniform(keys[5], (SHARDS, P_BLK, BLOCK), jnp.float32) ** block_levels(keys[5], (SHARDS, P_BLK, BLOCK), ((0, 32), (1, 4)), -0.2, 0.2)), 0.5, 50.0)
    return {"partials": partials, "worker_residual": worker_residual, "server_residual": server_residual, "master": master, "first_moment": first_moment, "second_moment": second_moment}


def reference(partials, worker_residual, server_residual, master, first_moment, second_moment):
    grouped = partials.reshape(PODS, SHARDS, BLOCKS, BLOCK)

    def pod_sum(group):

        def add_one(carry, piece):
            return (carry + piece.astype(jnp.float32), None)
        summed, unused = lax.scan(add_one, jnp.zeros((BLOCKS, BLOCK), jnp.float32), group)
        return summed
    pod_grad = lax.map(pod_sum, grouped)
    worker = pod_grad + worker_residual
    worker_scale = lax.optimization_barrier(jnp.max(jnp.abs(worker), axis=-1)) + 1e-06
    coded = (worker / worker_scale[..., None]).astype(jnp.bfloat16)
    total = lax.optimization_barrier(jnp.sum(coded.astype(jnp.float32) * worker_scale[..., None], axis=0))
    server = total + server_residual.reshape(BLOCKS, BLOCK)
    server_scale = lax.optimization_barrier(jnp.max(jnp.abs(server), axis=-1)) + 1e-06
    server_code = (server / server_scale[:, None]).astype(jnp.bfloat16)
    grad = (server_code.astype(jnp.float32) * server_scale[:, None]).reshape(SHARDS, P_BLK, BLOCK)
    new_first = 0.9 * first_moment + 0.1 * grad
    new_second = 0.95 * second_moment + 0.05 * grad * grad
    first_hat = new_first / (1.0 - 0.9 ** STEP)
    second_hat = new_second / (1.0 - 0.95 ** STEP)
    new_master = master - 0.01 * (first_hat / (jnp.sqrt(second_hat) + 1e-08) + 0.1 * master)
    params_full = new_master.astype(jnp.bfloat16).reshape(BLOCKS, BLOCK)
    return (new_master, new_first, new_second, params_full)
```

```python
import functools

import jax
import jax.numpy as jnp
from jax import lax
from jax.experimental import pallas as pl
from jax.experimental.pallas import tpu as pltpu
from jax.sharding import PartitionSpec as P

STEP = 10
MESH = pl.DeviceIdType.MESH
BF, F32 = jnp.bfloat16, jnp.float32
NX, NY, NH, NL, NC = 4, 4, 2, 2, 2
ROWS = 256

GROUPS = (64, 64, 64, 64)
EARLY = (("xyz", 0, 32), ("yxz", 32, 32))
LATE = (("xyz", 0, 16), ("yzx", 16, 16), ("zxy", 32, 16), ("yxz", 48, 16))
PARTS = (EARLY, EARLY, EARLY, LATE)
RELATIVE = [(b, h) for b in range(4) for h in range(2) if (b, h) != (0, 0)]


class At:
    def __init__(self):
        o, f = lax.axis_index("outer"), lax.axis_index("fsdp")
        self.o, self.f = o, f
        self.zl, self.c = o // 2, o % 2
        self.y, self.zh, self.x = f // 8, (f // 4) % 2, f % 4
        self.z = self.zh * 2 + self.zl

    def device(self, x=0, y=0, z=0, c=0):
        z = (self.z + z) % 4
        return {
            "outer": (z % 2) * 2 + (self.c + c) % 2,
            "fsdp": ((self.y + y) % 4) * 8 + (z // 2) * 4 + (self.x + x) % 4,
        }

    def pod(self, j):
        return (self.zl + j // 2) % 2, (self.c + j % 2) % 2


def partners():
    found = set()
    for b in range(1, 4):
        found |= {(b, 0, 0, 0), (0, b, 0, 0)}
    for b, h in RELATIVE:
        found |= {(b, 0, 2 * h, 0), (0, b, 2 * h, 0)}
    found |= {(0, 0, 1, 0), (0, 0, 3, 0), (0, 0, 2, 0), (0, 0, 0, 1)}
    return sorted(found)


class Copies:
    def __init__(self, send, recv):
        self.send, self.recv, self.n, self.started = send, recv, 0, []

    def __call__(self, src, dst, to):
        copy = pltpu.make_async_remote_copy(
            src_ref=src, dst_ref=dst, send_sem=self.send.at[self.n], recv_sem=self.recv.at[self.n],
            device_id=to, device_id_type=MESH,
        )
        self.n += 1
        copy.start()
        self.started.append(copy)
        return copy


def kernel(parts_hbm, wres_hbm, sres_hbm, mast_hbm, mom1_hbm, mom2_hbm, new_mast, new_first, new_second, full,
           grads, wres, own, got_a, sum32, sum16, got_b, deq, got_o, load_sem, send_sem, recv_sem):
    at = At()
    starts = [sum(GROUPS[:g]) for g in range(len(GROUPS))]
    rows = [pl.ds(s, r) for s, r in zip(starts, GROUPS)]
    n_groups = len(GROUPS)

    loads = []
    for g in range(n_groups):
        view = (slice(None),) * 4 + (rows[g],)
        loads.append(pltpu.make_async_copy(parts_hbm.at[view], grads.at[view], load_sem.at[g]))
    small = [
        pltpu.make_async_copy(src, dst, load_sem.at[n_groups + i])
        for i, (src, dst) in enumerate(
            [(wres_hbm, wres), (sres_hbm, own.at[0]), (mast_hbm, own.at[1]), (mom1_hbm, own.at[2]), (mom2_hbm, own.at[3])]
        )
    ]
    for copy in loads + small:
        copy.start()

    barrier = pltpu.get_barrier_semaphore()
    met = partners()
    for x, y, z, c in met:
        pl.semaphore_signal(barrier, inc=1, device_id=at.device(x, y, z, c), device_id_type=MESH)
    zl, c = at.pod(3)
    pl.semaphore_signal(barrier, inc=1, device_id={"outer": zl * 2 + c, "fsdp": at.f}, device_id_type=MESH)
    pl.semaphore_wait(barrier, len(met) + 1)

    send = Copies(send_sem, recv_sem)
    mine = (at.x, at.y)
    a, b, d, outs = {}, {}, {}, {}

    def chunk(g, s, to, h):
        if s == 0:
            return grads.at[:, h, to, 0:2, rows[g], :]
        return grads.at[to, h, :, 2:4, rows[g], :]

    def along(s, n):
        return at.device(x=n) if s == 0 else at.device(y=n)

    def a1(g):
        loads[g].wait()
        for s in range(2):
            i = mine[s]
            ahead, behind, across = (i + 1) % 4, (i + 3) % 4, (i + 2) % 4
            into = lambda k: got_a.at[s, k, :, :, rows[g], :]
            a[g, s] = [
                send(chunk(g, s, across, 0), into(0), along(s, 1)),
                send(chunk(g, s, across, 1), into(1), along(s, 3)),
                send(chunk(g, s, ahead, 1), into(2), along(s, 1)),
                send(chunk(g, s, behind, 0), into(3), along(s, 3)),
            ]

    def a2(g):
        for s in range(2):
            i = mine[s]
            into = lambda k: got_a.at[s, k, :, :, rows[g], :]
            for k, to, n in ((0, (i + 1) % 4, 1), (1, (i + 3) % 4, 3)):
                a[g, s][k].wait_recv()
                block = chunk(g, s, to, k)
                block[...] = (block[...].astype(F32) + into(k)[...].astype(F32)).astype(BF)
                a[g, s].append(send(block, into(4 + k), along(s, n)))

    def a3(g):
        for s in range(2):
            i, j = mine[s], mine[1 - s]
            into = lambda k: got_a.at[s, k, :, :, rows[g], :]
            for h, (k, m) in enumerate(((4, 3), (2, 5))):
                a[g, s][k].wait_recv()
                a[g, s][m].wait_recv()
                summed = chunk(g, s, i, h)[...].astype(F32) + into(k)[...].astype(F32) + into(m)[...].astype(F32)
                sum32[s, :, h, :, 0:GROUPS[g], :] = summed
                sum16[s, :, h, :, rows[g], :] = summed.astype(BF)
            b[g, s] = []
            for n, (db, dh) in enumerate(RELATIVE):
                to = along(1 - s, db) if dh == 0 else (at.device(y=db, z=2) if s == 0 else at.device(x=db, z=2))
                b[g, s].append(
                    send(sum16.at[s, (j + db) % 4, (at.zh + dh) % 2, :, rows[g], :], got_b.at[s, n, :, rows[g], :], to)
                )
            own_sum = sum32[s, j, at.zh, :, 0:GROUPS[g], :]
            deq[2 * s:2 * s + 2, rows[g], :] = own_sum

    def b1(g):
        for s in range(2):
            both = slice(2 * s, 2 * s + 2)
            pod_grad = deq[both, rows[g], :]
            for n, copy in enumerate(b[g, s]):
                copy.wait_recv()
                pod_grad = pod_grad + got_b[s, n, :, rows[g], :].astype(F32)
            worker = pod_grad + wres[both, rows[g], :]
            scale = jnp.max(jnp.abs(worker), axis=-1, keepdims=True) + 1e-06
            coded = (worker / scale).astype(BF)
            deq[both, rows[g], :] = coded.astype(F32) * scale
        d[g] = []
        for j in range(1, 4):
            zl, c = at.pod(j)
            d[g].append(send(deq.at[zl * 2 + c, rows[g], :], got_o.at[j - 1, rows[g], :], {"outer": zl * 2 + c, "fsdp": at.f}))

    def c1(g):
        total = deq[at.o, rows[g], :]
        for j in range(3):
            d[g][j].wait_recv()
            total = total + got_o[j, rows[g], :]
        server = total + own[0, rows[g], :]
        scale = jnp.max(jnp.abs(server), axis=-1, keepdims=True) + 1e-06
        code = (server / scale).astype(BF)
        grad = code.astype(F32) * scale
        first = 0.9 * own[2, rows[g], :] + 0.1 * grad
        second = 0.95 * own[3, rows[g], :] + 0.05 * grad * grad
        first_hat = first / (1.0 - 0.9**STEP)
        second_hat = second / (1.0 - 0.95**STEP)
        old = own[1, rows[g], :]
        new = old - 0.01 * (first_hat / (jnp.sqrt(second_hat) + 1e-08) + 0.1 * old)
        new_mast[rows[g], :] = new
        new_first[rows[g], :] = first
        new_second[rows[g], :] = second
        full[at.y, at.zh, at.x, at.zl, at.c, rows[g], :] = new.astype(BF)
        for p in range(len(PARTS[g])):
            gather_one(g, p, 0)

    def region(g, p, spread, halves=None):
        order, first, count = PARTS[g][p]
        pick = {"x": at.x, "y": at.y}
        for axis in spread:
            pick[axis] = slice(None)
        zh, zl = (slice(None), slice(None)) if "z" in spread else (at.zh, at.zl)
        if halves is not None:
            axis, offset, lead, half = halves
            if axis == "z":
                z = (at.z + offset) % 4
                zh, zl = z // 2, z % 2
            else:
                pick[axis] = ((at.x if axis == "x" else at.y) + offset) % 4
            if half is not None:
                if lead == "z":
                    zh = slice(half, half + 1)
                else:
                    pick[lead] = slice(2 * half, 2 * half + 2)
        return full.at[pick["y"], zh, pick["x"], zl, at.c, pl.ds(starts[g] + first, count), :]

    def to_axis(axis, n):
        return at.device(**{axis: n})

    sibling = at.device(c=1)
    cores = []

    def gather_one(g, p, stage):
        order = PARTS[g][p][0]
        key = (g, p)
        if stage > 0:
            for copy in outs[key]:
                copy.wait_recv()
        if stage < 2:
            piece = region(g, p, order[:stage])
            outs[key] = [send(piece, piece, to_axis(order[stage], n)) for n in (1, 3, 2)]
        elif stage == 2:
            piece = region(g, p, order[:2])
            outs[key] = [send(piece, piece, to_axis(order[2], n)) for n in (1, 3)]
            cores.append(send(piece, piece, sibling))
        elif stage == 3:
            back = region(g, p, order[:2], (order[2], 3, order[0], 0))
            front = region(g, p, order[:2], (order[2], 1, order[0], 1))
            outs[key] = [send(back, back, to_axis(order[2], 1)), send(front, front, to_axis(order[2], 3))]
            for n in (1, 3):
                piece = region(g, p, order[:2], (order[2], n, None, None))
                cores.append(send(piece, piece, sibling))
        else:
            piece = region(g, p, order[:2], (order[2], 2, None, None))
            cores.append(send(piece, piece, sibling))

    def gather(g, stage):
        for p in range(len(PARTS[g])):
            gather_one(g, p, stage)

    for copy in small:
        copy.wait()
    a1(0)
    for t in range(n_groups + 4):
        if t < n_groups:
            a2(t)
        if t + 1 < n_groups:
            a1(t + 1)
        if 0 <= t - 2 < n_groups:
            gather(t - 2, 1)
        if 0 <= t - 3 < n_groups:
            gather(t - 3, 3)
        if 0 <= t - 1 < n_groups:
            b1(t - 1)
        if 0 <= t - 2 < n_groups:
            gather(t - 2, 2)
        if t < n_groups:
            a3(t)
        if 0 <= t - 1 < n_groups:
            c1(t - 1)
        if 0 <= t - 3 < n_groups:
            gather(t - 3, 4)
    for copy in cores:
        copy.wait_recv()
    for copy in send.started:
        copy.wait_send()


def copies_needed():
    per_group = 2 * (6 + 7) + 3
    return len(GROUPS) * per_group + sum(len(p) for p in PARTS) * (3 + 3 + 2 + 1 + 2 + 2 + 1)


def local(partials, worker_residual, server_residual, master, first_moment, second_moment):
    grads = partials.reshape(NY, NH, NX, NL * NC, ROWS, 128)
    wres = worker_residual.reshape(NL * NC, ROWS, 128)
    flat = [v.reshape(ROWS, 128) for v in (server_residual, master, first_moment, second_moment)]
    n = copies_needed()
    any_space = pl.BlockSpec(memory_space=pl.ANY)
    vmem = pl.BlockSpec(memory_space=pltpu.VMEM)
    tall = max(GROUPS)
    shard = jax.ShapeDtypeStruct((ROWS, 128), F32)
    new_mast, new_first, new_second, full = pl.pallas_call(
        kernel,
        out_shape=(shard, shard, shard, pltpu.VMEM((NY, NH, NX, NL, NC, ROWS, 128), BF)),
        in_specs=[any_space] * 6,
        out_specs=(vmem,) * 4,
        scratch_shapes=[
            pltpu.VMEM((NY, NH, NX, NL * NC, ROWS, 128), BF),
            pltpu.VMEM((NL * NC, ROWS, 128), F32),
            pltpu.VMEM((4, ROWS, 128), F32),
            pltpu.VMEM((2, 6, 4, 2, ROWS, 128), BF),
            pltpu.VMEM((2, 4, 2, 2, tall, 128), F32),
            pltpu.VMEM((2, 4, 2, 2, ROWS, 128), BF),
            pltpu.VMEM((2, 7, 2, ROWS, 128), BF),
            pltpu.VMEM((4, ROWS, 128), F32),
            pltpu.VMEM((3, ROWS, 128), F32),
            pltpu.SemaphoreType.DMA((len(GROUPS) + 5,)),
            pltpu.SemaphoreType.DMA((n,)),
            pltpu.SemaphoreType.DMA((n,)),
        ],
        compiler_params=pltpu.CompilerParams(collective_id=0, has_side_effects=True, vmem_limit_bytes=44 * 2**20),
    )(grads, wres, *flat)
    return new_mast[None], new_first[None], new_second[None], full.reshape(NY * NH * NX * NL * NC * ROWS, 128)


def solution(mesh):
    placed = (
        P(("outer", "fsdp"), None, None),
        P("outer", "fsdp", None),
        P("fsdp", "outer", None),
        P("fsdp", "outer", None),
        P("fsdp", "outer", None),
        P("fsdp", "outer", None),
    )
    return jax.shard_map(
        local,
        mesh=mesh,
        in_specs=placed,
        out_specs=(P("fsdp", "outer", None), P("fsdp", "outer", None), P("fsdp", "outer", None), P()),
        check_vma=False,
    )
```

```python
import functools

import jax
import jax.numpy as jnp
from jax import lax
from jax.experimental import pallas as pl
from jax.experimental.pallas import tpu as pltpu
from jax.sharding import PartitionSpec as P

STEP = 10
MESH = pl.DeviceIdType.MESH
BF, F32 = jnp.bfloat16, jnp.float32
NX, NY, NH, NL, NC = 4, 4, 2, 2, 2
ROWS = 256

GROUPS = (("n", 64), ("n", 64), ("n", 64), ("z", 32), ("z", 32))
BATCHES = (
    ((0, 1, 2), (("xyz", 0, 64), ("yzx", 64, 64), ("zxy", 128, 64))),
    ((3, 4), (("xyz", 192, 16), ("yzx", 208, 16), ("zxy", 224, 32))),
)
TIMES = (
    {"a1": -9, "a2": 5.5, "a3": 12, "b": 18, "c": 24, "d": 29},
    {"a1": -8, "a2": 14, "a3": 21, "b": 27, "c": 33, "d": 38},
    {"a1": 7, "a2": 23, "a3": 30, "b": 36, "c": 42, "d": 47},
    {"z1": -7, "z2": 14, "a2": 20, "a3": 25, "b": 31, "d": 36},
    {"z1": -6, "z2": 24.5, "a2": 32, "a3": 37, "b": 41, "d": 45},
)
GATHER_TIMES = (
    {"g1": 51, "g2": 55, "g3": 60, "g4": 64},
    {"g1": 52, "g2": 56, "g3": 61, "g4": 65},
)


class At:
    def __init__(self):
        o, f = lax.axis_index("outer"), lax.axis_index("fsdp")
        self.o, self.f = o, f
        self.zl, self.c = o // 2, o % 2
        self.y, self.zh, self.x = f // 8, (f // 4) % 2, f % 4
        self.z = self.zh * 2 + self.zl

    def device(self, x=0, y=0, z=0, c=0):
        z = (self.z + z) % 4
        return {
            "outer": (z % 2) * 2 + (self.c + c) % 2,
            "fsdp": ((self.y + y) % 4) * 8 + (z // 2) * 4 + (self.x + x) % 4,
        }

    def pod(self, j):
        return (self.zl + j // 2) % 2, (self.c + j % 2) % 2


def partners():
    found = {(0, 0, 0, 1)}
    for b in range(1, 4):
        found |= {(b, 0, 0, 0), (0, b, 0, 0), (0, 0, b, 0)}
    return sorted(found)


class Copies:
    def __init__(self, send, recv):
        self.send, self.recv, self.n, self.started = send, recv, 0, []

    def __call__(self, src, dst, to):
        copy = pltpu.make_async_remote_copy(
            src_ref=src, dst_ref=dst, send_sem=self.send.at[self.n], recv_sem=self.recv.at[self.n],
            device_id=to, device_id_type=MESH,
        )
        self.n += 1
        copy.start()
        self.started.append(copy)
        return copy


def kernel(parts_hbm, wres_hbm, sres_hbm, mast_hbm, mom1_hbm, mom2_hbm, new_mast, new_first, new_second, full,
           grads, wres, own, got_a, got_z, sum32, sum16, own32, got_b, out16, got_c, deq, got_o,
           load_sem, send_sem, recv_sem):
    at = At()
    n_groups = len(GROUPS)
    kinds = [kind for kind, _ in GROUPS]
    sizes = [r for _, r in GROUPS]
    rows = [pl.ds(sum(sizes[:g]), r) for g, r in enumerate(sizes)]
    z_from = sum(r for kind, r in GROUPS if kind == "n")

    loads = []
    for g in range(n_groups):
        view = (slice(None),) * 4 + (rows[g],)
        loads.append(pltpu.make_async_copy(parts_hbm.at[view], grads.at[view], load_sem.at[g]))
    small = [
        pltpu.make_async_copy(src, dst, load_sem.at[n_groups + i])
        for i, (src, dst) in enumerate(
            [(wres_hbm, wres), (sres_hbm, own.at[0]), (mast_hbm, own.at[1]), (mom1_hbm, own.at[2]), (mom2_hbm, own.at[3])]
        )
    ]
    for copy in loads + small:
        copy.start()

    barrier = pltpu.get_barrier_semaphore()
    met = partners()
    for x, y, z, c in met:
        pl.semaphore_signal(barrier, inc=1, device_id=at.device(x, y, z, c), device_id_type=MESH)
    zl, c = at.pod(3)
    pl.semaphore_signal(barrier, inc=1, device_id={"outer": zl * 2 + c, "fsdp": at.f}, device_id_type=MESH)
    pl.semaphore_wait(barrier, len(met) + 1)

    send = Copies(send_sem, recv_sem)
    mine = (at.x, at.y)
    a, b, c_, d, z = {}, {}, {}, {}, {}

    def chunk(g, s, to, h):
        if kinds[g] == "n":
            return grads.at[:, h, to, 0:2, rows[g], :] if s == 0 else grads.at[to, h, :, 2:4, rows[g], :]
        if s == 0:
            return grads.at[:, at.zh, to, h:h + 1, rows[g], :]
        return grads.at[to, at.zh, :, 2 + h:3 + h, rows[g], :]

    def along(s, n):
        return at.device(x=n) if s == 0 else at.device(y=n)

    def into(g, s, k):
        return got_a.at[s, k, :, 0:(2 if kinds[g] == "n" else 1), rows[g], :]

    def ring(g):
        for s in range(2):
            i = mine[s]
            ahead, behind, across = (i + 1) % 4, (i + 3) % 4, (i + 2) % 4
            a[g, s] = [
                send(chunk(g, s, across, 0), into(g, s, 0), along(s, 1)),
                send(chunk(g, s, across, 1), into(g, s, 1), along(s, 3)),
                send(chunk(g, s, ahead, 1), into(g, s, 2), along(s, 1)),
                send(chunk(g, s, behind, 0), into(g, s, 3), along(s, 3)),
            ]

    def a1(g):
        loads[g].wait()
        ring(g)

    def z_rows(g):
        return pl.ds(sum(sizes[:g]) - z_from, sizes[g])

    def z1(g):
        loads[g].wait()
        z[g] = send(grads.at[:, 1 - at.zh, :, :, rows[g], :], got_z.at[:, :, :, z_rows(g), :], at.device(z=2))

    def z2(g):
        z[g].wait_recv()
        for y in range(NY):
            block = grads.at[y, at.zh, :, :, rows[g], :]
            block[...] = (block[...].astype(F32) + got_z[y, :, :, z_rows(g), :].astype(F32)).astype(BF)
        ring(g)

    def a2(g):
        for s in range(2):
            i = mine[s]
            for k, to, n in ((0, (i + 1) % 4, 1), (1, (i + 3) % 4, 3)):
                a[g, s][k].wait_recv()
                block = chunk(g, s, to, k)
                block[...] = (block[...].astype(F32) + into(g, s, k)[...].astype(F32)).astype(BF)
                a[g, s].append(send(block, into(g, s, 4 + k), along(s, n)))

    def a3(g):
        nz = 2 if kinds[g] == "n" else 1
        for s in range(2):
            i, j = mine[s], mine[1 - s]
            for h, (k, m) in enumerate(((4, 3), (2, 5))):
                a[g, s][k].wait_recv()
                a[g, s][m].wait_recv()
                summed = chunk(g, s, i, h)[...].astype(F32) + into(g, s, k)[...].astype(F32) + into(g, s, m)[...].astype(F32)
                if nz == 2:
                    sum32[s, :, h, :, 0:sizes[g], :] = summed
                    sum16[s, :, h, :, rows[g], :] = summed.astype(BF)
                else:
                    sum32[s, :, 0, h:h + 1, 0:sizes[g], :] = summed
                    sum16[s, :, 0, h:h + 1, rows[g], :] = summed.astype(BF)
            b[g, s] = [
                send(sum16.at[s, (j + n) % 4, 0:nz, :, rows[g], :], got_b.at[s, n - 1, 0:nz, :, rows[g], :], along(1 - s, n))
                for n in (1, 3, 2)
            ]
            own32[s, 0:nz, :, rows[g], :] = sum32[s, j, 0:nz, :, 0:sizes[g], :]

    def b1(g):
        for s in range(2):
            for copy in b[g, s]:
                copy.wait_recv()

            def second(h):
                total = own32[s, h, :, rows[g], :]
                for n in range(3):
                    total = total + got_b[s, n, h, :, rows[g], :].astype(F32)
                return total

            both = slice(2 * s, 2 * s + 2)
            if kinds[g] == "n":
                out16[both, rows[g], :] = second(1 - at.zh).astype(BF)
                deq[both, rows[g], :] = second(at.zh)
            else:
                deq[both, rows[g], :] = second(0)
        if kinds[g] == "n":
            c_[g] = send(out16.at[:, rows[g], :], got_c.at[:, rows[g], :], at.device(z=2))
        else:
            code(g, deq[:, rows[g], :])

    def c1(g):
        c_[g].wait_recv()
        code(g, deq[:, rows[g], :] + got_c[:, rows[g], :].astype(F32))

    def code(g, pod_grad):
        worker = pod_grad + wres[:, rows[g], :]
        scale = jnp.max(jnp.abs(worker), axis=-1, keepdims=True) + 1e-06
        coded = (worker / scale).astype(BF)
        deq[:, rows[g], :] = coded.astype(F32) * scale
        d[g] = []
        for j in range(1, 4):
            zl, c = at.pod(j)
            d[g].append(send(deq.at[zl * 2 + c, rows[g], :], got_o.at[j - 1, rows[g], :], {"outer": zl * 2 + c, "fsdp": at.f}))

    def d1(g):
        total = deq[at.o, rows[g], :]
        for j in range(3):
            d[g][j].wait_recv()
            total = total + got_o[j, rows[g], :]
        server = total + own[0, rows[g], :]
        scale = jnp.max(jnp.abs(server), axis=-1, keepdims=True) + 1e-06
        server_code = (server / scale).astype(BF)
        grad = server_code.astype(F32) * scale
        first = 0.9 * own[2, rows[g], :] + 0.1 * grad
        second = 0.95 * own[3, rows[g], :] + 0.05 * grad * grad
        first_hat = first / (1.0 - 0.9**STEP)
        second_hat = second / (1.0 - 0.95**STEP)
        old = own[1, rows[g], :]
        new = old - 0.01 * (first_hat / (jnp.sqrt(second_hat) + 1e-08) + 0.1 * old)
        new_mast[rows[g], :] = new
        new_first[rows[g], :] = first
        new_second[rows[g], :] = second
        full[at.y, at.zh, at.x, at.zl, at.c, rows[g], :] = new.astype(BF)

    def region(part, along_a=None, at_b=0, at_c=0):
        order, first, count = part
        here = {"x": at.x, "y": at.y, "z": at.z}
        pick = {order[1]: (here[order[1]] + at_b) % 4, order[2]: (here[order[2]] + at_c) % 4}
        if along_a == "own":
            pick[order[0]] = here[order[0]]
        if "z" in pick:
            zh, zl = pick["z"] // 2, pick["z"] % 2
        else:
            zh, zl = (slice(None) if along_a is None else slice(along_a, along_a + 1)), slice(None)
        for axis in "xy":
            if axis not in pick:
                pick[axis] = slice(None) if along_a is None else slice(2 * along_a, 2 * along_a + 2)
        return full.at[pick["y"], zh, pick["x"], zl, at.c, pl.ds(first, count), :]

    def to_axis(axis, n):
        return at.device(**{axis: n})

    sibling = at.device(c=1)
    cores, ga, gb, gc, gd = [], {}, {}, {}, {}

    def twin(part, *at_):
        piece = region(part, None, *at_)
        cores.append(send(piece, piece, sibling))

    def third(part, at_b):
        piece = region(part, None, at_b)
        gc[part, at_b] = [send(piece, piece, to_axis(part[0][2], n)) for n in (1, 3)]

    def g0(parts):
        for part in parts:
            piece = region(part, "own")
            ga[part] = [send(piece, piece, to_axis(part[0][0], n)) for n in (1, 3, 2)]

    def g1(parts):
        for part in parts:
            for copy in ga[part]:
                copy.wait_recv()
            piece = region(part)
            gb[part] = [send(piece, piece, to_axis(part[0][1], n)) for n in (1, 3, 2)]
            third(part, 0)

    def g2(parts):
        for i, at_b in enumerate((3, 1, 2)):
            for part in parts:
                gb[part][i].wait_recv()
                third(part, at_b)
        for part in parts:
            for at_b in range(4):
                twin(part, at_b)

    def g3(parts):
        for at_b in (0, 3, 1, 2):
            for part in parts:
                axis = part[0][2]
                for copy in gc[part, at_b]:
                    copy.wait_recv()
                back, front = region(part, 0, at_b, 3), region(part, 1, at_b, 1)
                gd[part, at_b] = [send(back, back, to_axis(axis, 1)), send(front, front, to_axis(axis, 3))]
                twin(part, at_b, 1)
                twin(part, at_b, 3)

    def g4(parts):
        for at_b in (0, 3, 1, 2):
            for part in parts:
                for copy in gd[part, at_b]:
                    copy.wait_recv()
                twin(part, at_b, 2)

    steps = {"a1": a1, "a2": a2, "a3": a3, "z1": z1, "z2": z2, "b": b1, "c": c1, "d": d1}
    gathers = {"g0": g0, "g1": g1, "g2": g2, "g3": g3, "g4": g4}
    for copy in small:
        copy.wait()
    for name, n in schedule():
        if name in steps:
            steps[name](n)
        else:
            gathers[name](BATCHES[n][1])
    for copy in cores:
        copy.wait_recv()
    for copy in send.started:
        copy.wait_send()


def schedule():
    order = [(t, 0, name, g) for g, times in enumerate(TIMES) for name, t in times.items()]
    order += [(t, 1, name, n) for n, times in enumerate(GATHER_TIMES) for name, t in times.items()]
    for n, (groups, _) in enumerate(BATCHES):
        order.append((max(TIMES[g]["d"] for g in groups), 1, "g0", n))
    return [(name, n) for _, _, name, n in sorted(order)]


def write_out(*refs):
    n = len(refs) // 2
    sem = refs[-1]
    copies = [pltpu.make_async_copy(refs[i], refs[n + i], sem.at[i]) for i in range(n)]
    for copy in copies:
        copy.start()
    for copy in copies:
        copy.wait()


def copies_needed():
    per_group = {"n": 2 * (6 + 3) + 1 + 3, "z": 1 + 2 * (6 + 3) + 3}
    per_part = 3 + 3 + 4 * (2 + 2 + 4)
    return sum(per_group[kind] for kind, _ in GROUPS) + per_part * sum(len(parts) for _, parts in BATCHES)


def local(partials, worker_residual, server_residual, master, first_moment, second_moment):
    grads = partials.reshape(NY, NH, NX, NL * NC, ROWS, 128)
    wres = worker_residual.reshape(NL * NC, ROWS, 128)
    flat = [v.reshape(ROWS, 128) for v in (server_residual, master, first_moment, second_moment)]
    n = copies_needed()
    hbm = pl.BlockSpec(memory_space=pltpu.HBM)
    vmem = pl.BlockSpec(memory_space=pltpu.VMEM)
    tall = max(r for _, r in GROUPS)
    z_rows = sum(r for kind, r in GROUPS if kind == "z")
    shard = pltpu.VMEM((ROWS, 128), F32)
    results = pl.pallas_call(
        kernel,
        out_shape=(shard, shard, shard, pltpu.VMEM((NY, NH, NX, NL, NC, ROWS, 128), BF)),
        in_specs=[hbm] * 6,
        out_specs=(vmem,) * 4,
        scratch_shapes=[
            pltpu.VMEM((NY, NH, NX, NL * NC, ROWS, 128), BF),
            pltpu.VMEM((NL * NC, ROWS, 128), F32),
            pltpu.VMEM((4, ROWS, 128), F32),
            pltpu.VMEM((2, 6, 4, 2, ROWS, 128), BF),
            pltpu.VMEM((NY, NX, NL * NC, max(z_rows, 16), 128), BF),
            pltpu.VMEM((2, 4, 2, 2, tall, 128), F32),
            pltpu.VMEM((2, 4, 2, 2, ROWS, 128), BF),
            pltpu.VMEM((2, 2, 2, ROWS, 128), F32),
            pltpu.VMEM((2, 3, 2, 2, ROWS, 128), BF),
            pltpu.VMEM((NL * NC, ROWS, 128), BF),
            pltpu.VMEM((NL * NC, ROWS, 128), BF),
            pltpu.VMEM((NL * NC, ROWS, 128), F32),
            pltpu.VMEM((3, ROWS, 128), F32),
            pltpu.SemaphoreType.DMA((len(GROUPS) + 5,)),
            pltpu.SemaphoreType.DMA((n,)),
            pltpu.SemaphoreType.DMA((n,)),
        ],
        compiler_params=pltpu.CompilerParams(collective_id=0, has_side_effects=True, vmem_limit_bytes=44 * 2**20),
    )(*[pltpu.with_memory_space_constraint(v, pltpu.HBM) for v in (grads, wres, *flat)])
    new_mast, new_first, new_second, full = pl.pallas_call(
        write_out,
        out_shape=[jax.ShapeDtypeStruct(v.shape, v.dtype) for v in results],
        in_specs=[pl.BlockSpec(memory_space=pl.ANY)] * 4,
        out_specs=[pl.BlockSpec(memory_space=pl.ANY)] * 4,
        scratch_shapes=[pltpu.SemaphoreType.DMA((4,))],
        compiler_params=pltpu.CompilerParams(vmem_limit_bytes=2**20),
    )(*[pltpu.with_memory_space_constraint(v, pltpu.VMEM) for v in results])
    return new_mast[None], new_first[None], new_second[None], full.reshape(NY * NH * NX * NL * NC * ROWS, 128)


def solution(mesh):
    placed = (
        P(("outer", "fsdp"), None, None),
        P("outer", "fsdp", None),
        P("fsdp", "outer", None),
        P("fsdp", "outer", None),
        P("fsdp", "outer", None),
        P("fsdp", "outer", None),
    )
    return jax.shard_map(
        local,
        mesh=mesh,
        in_specs=placed,
        out_specs=(P("fsdp", "outer", None), P("fsdp", "outer", None), P("fsdp", "outer", None), P()),
        check_vma=False,
    )
```

```python
import functools

import jax
import jax.numpy as jnp
from jax import lax
from jax.experimental import pallas as pl
from jax.experimental.pallas import tpu as pltpu
from jax.sharding import PartitionSpec as P

STEP = 10
MESH = pl.DeviceIdType.MESH
BF, F32 = jnp.bfloat16, jnp.float32
NX, NY, NH, NL, NC = 4, 4, 2, 2, 2
ROWS = 256

GROUPS = (("n", 48), ("n", 32), ("z", 32), ("z", 32), ("n", 96), ("z", 16))
BATCHES = (
    ((0,), (("yzx", 0, 16, 0, 0),)),
    ((0,), (("yzx", 16, 16, 0, 0),)),
    ((0,), (("yxz", 32, 16, 0, 1),)),
    ((1, 2), (("xzy", 48, 48, 0, 0),)),
    ((1, 2), (("xyz", 96, 16, 0, 0),)),
    ((3,), (("yxz", 112, 16, 0, 0),)),
    ((3,), (("xyz", 128, 16, 0, 0),)),
    ((4,), (("yzx", 144, 48, 0, 0), ("zxy", 192, 32, 0, 0), ("xyz", 224, 16, 1, 0))),
    ((5,), (("xzy", 240, 16, 0, 0),)),
)
ORDER = (
    ("z1", 2), ("a1", 4), ("a1", 1), ("a2", 4), ("z1", 3), ("a2", 1), ("a1", 0), ("a3", 4),
    ("z2", 2), ("a3", 1), ("z1", 5), ("a2", 0), ("z2", 3), ("a2", 2), ("b", 4), ("z2", 5),
    ("b", 1), ("a3", 0), ("a2", 3), ("a3", 2), ("c", 4), ("a2", 5), ("c", 1), ("a3", 3),
    ("b", 0), ("a3", 5), ("b", 2), ("d", 4), ("d", 1), ("g0", 7), ("b", 3), ("b", 5),
    ("d", 2), ("c", 0), ("g0", 3), ("g0", 4), ("g1", 7), ("d", 3), ("d", 5), ("g0", 5),
    ("g0", 6), ("g0", 8), ("d", 0), ("g1", 3), ("g0", 0), ("g0", 1), ("g0", 2), ("g1", 4),
    ("g1", 5), ("g1", 6), ("g1", 8), ("g2", 7), ("g1", 0), ("g1", 1), ("g1", 2), ("g2", 4),
    ("g2", 3), ("g2", 5), ("g2", 6), ("g2", 8), ("g2", 0), ("g2", 1), ("g3", 4), ("g3", 7),
    ("g3", 5), ("g2", 2), ("g3", 0), ("g3", 6), ("g3", 3), ("g4", 4), ("g3", 1), ("g3", 8),
    ("g4", 5), ("g4", 7), ("g3", 2), ("g4", 0), ("g4", 1), ("g4", 3), ("g4", 6), ("g4", 2),
    ("g4", 8),
)


class At:
    def __init__(self):
        o, f = lax.axis_index("outer"), lax.axis_index("fsdp")
        self.o, self.f = o, f
        self.zl, self.c = o // 2, o % 2
        self.y, self.zh, self.x = f // 8, (f // 4) % 2, f % 4
        self.z = self.zh * 2 + self.zl

    def device(self, x=0, y=0, z=0, c=0):
        z = (self.z + z) % 4
        return {
            "outer": (z % 2) * 2 + (self.c + c) % 2,
            "fsdp": ((self.y + y) % 4) * 8 + (z // 2) * 4 + (self.x + x) % 4,
        }

    def pod(self, j):
        return (self.zl + j // 2) % 2, (self.c + j % 2) % 2


def partners():
    found = {(0, 0, 0, 1)}
    for b in range(1, 4):
        found |= {(b, 0, 0, 0), (0, b, 0, 0), (0, 0, b, 0)}
    return sorted(found)


class Copies:
    def __init__(self, send, recv):
        self.send, self.recv, self.n, self.started = send, recv, 0, []

    def __call__(self, src, dst, to):
        copy = pltpu.make_async_remote_copy(
            src_ref=src, dst_ref=dst, send_sem=self.send.at[self.n], recv_sem=self.recv.at[self.n],
            device_id=to, device_id_type=MESH,
        )
        self.n += 1
        copy.start()
        self.started.append(copy)
        return copy


def kernel(parts_hbm, wres_hbm, sres_hbm, mast_hbm, mom1_hbm, mom2_hbm, new_mast, new_first, new_second, full,
           grads, wres, own, got_a, got_z, sum32, sum16, own32, got_b, out16, got_c, deq, got_o,
           load_sem, send_sem, recv_sem):
    at = At()
    n_groups = len(GROUPS)
    kinds = [kind for kind, _ in GROUPS]
    sizes = [r for _, r in GROUPS]
    rows = [pl.ds(sum(sizes[:g]), r) for g, r in enumerate(sizes)]

    loads = []
    for g in range(n_groups):
        view = (slice(None),) * 4 + (rows[g],)
        loads.append(pltpu.make_async_copy(parts_hbm.at[view], grads.at[view], load_sem.at[g]))
    small = [
        pltpu.make_async_copy(src, dst, load_sem.at[n_groups + i])
        for i, (src, dst) in enumerate(
            [(wres_hbm, wres), (sres_hbm, own.at[0]), (mast_hbm, own.at[1]), (mom1_hbm, own.at[2]), (mom2_hbm, own.at[3])]
        )
    ]
    for copy in loads + small:
        copy.start()

    barrier = pltpu.get_barrier_semaphore()
    met = partners()
    for x, y, z, c in met:
        pl.semaphore_signal(barrier, inc=1, device_id=at.device(x, y, z, c), device_id_type=MESH)
    zl, c = at.pod(3)
    pl.semaphore_signal(barrier, inc=1, device_id={"outer": zl * 2 + c, "fsdp": at.f}, device_id_type=MESH)
    pl.semaphore_wait(barrier, len(met) + 1)

    send = Copies(send_sem, recv_sem)
    mine = (at.x, at.y)
    a, b, c_, d, z = {}, {}, {}, {}, {}

    def chunk(g, s, to, h):
        if kinds[g] == "n":
            return grads.at[:, h, to, 0:2, rows[g], :] if s == 0 else grads.at[to, h, :, 2:4, rows[g], :]
        if s == 0:
            return grads.at[:, at.zh, to, h:h + 1, rows[g], :]
        return grads.at[to, at.zh, :, 2 + h:3 + h, rows[g], :]

    def along(s, n):
        return at.device(x=n) if s == 0 else at.device(y=n)

    def into(g, s, k):
        return got_a.at[s, k, :, 0:(2 if kinds[g] == "n" else 1), rows[g], :]

    def ring(g):
        for s in range(2):
            i = mine[s]
            ahead, behind, across = (i + 1) % 4, (i + 3) % 4, (i + 2) % 4
            a[g, s] = [
                send(chunk(g, s, across, 0), into(g, s, 0), along(s, 1)),
                send(chunk(g, s, across, 1), into(g, s, 1), along(s, 3)),
                send(chunk(g, s, ahead, 1), into(g, s, 2), along(s, 1)),
                send(chunk(g, s, behind, 0), into(g, s, 3), along(s, 3)),
            ]

    def a1(g):
        loads[g].wait()
        ring(g)

    def z_rows(g):
        return pl.ds(sum(r for kind, r in GROUPS[:g] if kind == "z"), sizes[g])

    def z1(g):
        loads[g].wait()
        z[g] = send(grads.at[:, 1 - at.zh, :, :, rows[g], :], got_z.at[:, :, :, z_rows(g), :], at.device(z=2))

    def z2(g):
        z[g].wait_recv()
        for y in range(NY):
            block = grads.at[y, at.zh, :, :, rows[g], :]
            block[...] = (block[...].astype(F32) + got_z[y, :, :, z_rows(g), :].astype(F32)).astype(BF)
        ring(g)

    def a2(g):
        for s in range(2):
            i = mine[s]
            for k, to, n in ((0, (i + 1) % 4, 1), (1, (i + 3) % 4, 3)):
                a[g, s][k].wait_recv()
                block = chunk(g, s, to, k)
                block[...] = (block[...].astype(F32) + into(g, s, k)[...].astype(F32)).astype(BF)
                a[g, s].append(send(block, into(g, s, 4 + k), along(s, n)))

    def a3(g):
        nz = 2 if kinds[g] == "n" else 1
        for s in range(2):
            i, j = mine[s], mine[1 - s]
            for h, (k, m) in enumerate(((4, 3), (2, 5))):
                a[g, s][k].wait_recv()
                a[g, s][m].wait_recv()
                summed = chunk(g, s, i, h)[...].astype(F32) + into(g, s, k)[...].astype(F32) + into(g, s, m)[...].astype(F32)
                if nz == 2:
                    sum32[s, :, h, :, 0:sizes[g], :] = summed
                    sum16[s, :, h, :, rows[g], :] = summed.astype(BF)
                else:
                    sum32[s, :, 0, h:h + 1, 0:sizes[g], :] = summed
                    sum16[s, :, 0, h:h + 1, rows[g], :] = summed.astype(BF)
            b[g, s] = [
                send(sum16.at[s, (j + n) % 4, 0:nz, :, rows[g], :], got_b.at[s, n - 1, 0:nz, :, rows[g], :], along(1 - s, n))
                for n in (1, 3, 2)
            ]
            own32[s, 0:nz, :, rows[g], :] = sum32[s, j, 0:nz, :, 0:sizes[g], :]

    def b1(g):
        for s in range(2):
            for copy in b[g, s]:
                copy.wait_recv()

            def second(h):
                total = own32[s, h, :, rows[g], :]
                for n in range(3):
                    total = total + got_b[s, n, h, :, rows[g], :].astype(F32)
                return total

            both = slice(2 * s, 2 * s + 2)
            if kinds[g] == "n":
                out16[both, rows[g], :] = second(1 - at.zh).astype(BF)
                deq[both, rows[g], :] = second(at.zh)
            else:
                deq[both, rows[g], :] = second(0)
        if kinds[g] == "n":
            c_[g] = send(out16.at[:, rows[g], :], got_c.at[:, rows[g], :], at.device(z=2))
        else:
            code(g, deq[:, rows[g], :])

    def c1(g):
        c_[g].wait_recv()
        code(g, deq[:, rows[g], :] + got_c[:, rows[g], :].astype(F32))

    def code(g, pod_grad):
        worker = pod_grad + wres[:, rows[g], :]
        scale = jnp.max(jnp.abs(worker), axis=-1, keepdims=True) + 1e-06
        coded = (worker / scale).astype(BF)
        deq[:, rows[g], :] = coded.astype(F32) * scale
        d[g] = []
        for j in range(1, 4):
            zl, c = at.pod(j)
            d[g].append(send(deq.at[zl * 2 + c, rows[g], :], got_o.at[j - 1, rows[g], :], {"outer": zl * 2 + c, "fsdp": at.f}))

    def d1(g):
        total = deq[at.o, rows[g], :]
        for j in range(3):
            d[g][j].wait_recv()
            total = total + got_o[j, rows[g], :]
        server = total + own[0, rows[g], :]
        scale = jnp.max(jnp.abs(server), axis=-1, keepdims=True) + 1e-06
        server_code = (server / scale).astype(BF)
        grad = server_code.astype(F32) * scale
        first = 0.9 * own[2, rows[g], :] + 0.1 * grad
        second = 0.95 * own[3, rows[g], :] + 0.05 * grad * grad
        first_hat = first / (1.0 - 0.9**STEP)
        second_hat = second / (1.0 - 0.95**STEP)
        old = own[1, rows[g], :]
        new = old - 0.01 * (first_hat / (jnp.sqrt(second_hat) + 1e-08) + 0.1 * old)
        new_mast[rows[g], :] = new
        new_first[rows[g], :] = first
        new_second[rows[g], :] = second
        full[at.y, at.zh, at.x, at.zl, at.c, rows[g], :] = new.astype(BF)

    def region(part, along_a=None, at_b=None, at_c=0):
        order, first, count = part[:3]
        here = {"x": at.x, "y": at.y, "z": at.z}
        pick = {order[2]: (here[order[2]] + at_c) % 4}
        if at_b is not None:
            pick[order[1]] = (here[order[1]] + at_b) % 4
        if along_a == "own":
            pick[order[0]] = here[order[0]]
        every = slice(None)
        half = order[0] if along_a in (0, 1) else None
        if "z" in pick:
            zh, zl = pick["z"] // 2, pick["z"] % 2
        else:
            zh, zl = (slice(along_a, along_a + 1) if half == "z" else every), every
        for axis in "xy":
            if axis not in pick:
                pick[axis] = slice(2 * along_a, 2 * along_a + 2) if half == axis else every
        return full.at[pick["y"], zh, pick["x"], zl, at.c, pl.ds(first, count), :]

    def to_axis(axis, n):
        return at.device(**{axis: n})

    sibling = at.device(c=1)
    cores, ga, gb, gc, gd = [], {}, {}, {}, {}

    def twin(part, *at_):
        piece = region(part, None, *at_)
        cores.append(send(piece, piece, sibling))

    def third(part, at_b):
        piece = region(part, None, at_b)
        gc[part, at_b] = [send(piece, piece, to_axis(part[0][2], n)) for n in (1, 3)]
        if part[4]:
            gd[part, at_b] = [send(piece, piece, to_axis(part[0][2], 2))]

    def blocks(part):
        return (0, 3, 1, 2) if part[3] else (None,)

    def g0(parts):
        for part in parts:
            piece = region(part, "own", 0)
            ga[part] = [send(piece, piece, to_axis(part[0][0], n)) for n in (1, 3, 2)]

    def g1(parts):
        for part in parts:
            for copy in ga[part]:
                copy.wait_recv()
            piece = region(part, None, 0)
            gb[part] = [send(piece, piece, to_axis(part[0][1], n)) for n in (1, 3, 2)]
            if part[3]:
                third(part, 0)

    def g2(parts):
        for i, at_b in enumerate((3, 1, 2)):
            for part in parts:
                gb[part][i].wait_recv()
                if part[3]:
                    third(part, at_b)
                elif i == 2:
                    third(part, None)
        for part in parts:
            for at_b in blocks(part):
                twin(part, at_b)

    def g3(parts):
        for i in range(4):
            for part in parts:
                if i >= len(blocks(part)):
                    continue
                at_b, axis = blocks(part)[i], part[0][2]
                for copy in gc[part, at_b]:
                    copy.wait_recv()
                if not part[4]:
                    back, front = region(part, 0, at_b, 3), region(part, 1, at_b, 1)
                    gd[part, at_b] = [send(back, back, to_axis(axis, 1)), send(front, front, to_axis(axis, 3))]
                twin(part, at_b, 1)
                twin(part, at_b, 3)

    def g4(parts):
        for i in range(4):
            for part in parts:
                if i >= len(blocks(part)):
                    continue
                at_b = blocks(part)[i]
                for copy in gd[part, at_b]:
                    copy.wait_recv()
                twin(part, at_b, 2)

    steps = {"a1": a1, "a2": a2, "a3": a3, "z1": z1, "z2": z2, "b": b1, "c": c1, "d": d1}
    gathers = {"g0": g0, "g1": g1, "g2": g2, "g3": g3, "g4": g4}
    for copy in small:
        copy.wait()
    for name, n in ORDER:
        if name in steps:
            steps[name](n)
        else:
            gathers[name](BATCHES[n][1])
    for copy in cores:
        copy.wait_recv()
    for copy in send.started:
        copy.wait_send()


def write_out(*refs):
    n = len(refs) // 2
    sem = refs[-1]
    pairs = [(refs[i], refs[n + i]) for i in range(n - 1)]
    pairs += [(refs[n - 1].at[y, h], refs[2 * n - 1].at[y, h]) for y in range(NY) for h in range(NH)]
    copies = [pltpu.make_async_copy(src, dst, sem.at[i]) for i, (src, dst) in enumerate(pairs)]
    for copy in copies:
        copy.start()
    for copy in copies:
        copy.wait()


def copies_needed():
    per_group = {"n": 2 * (6 + 3) + 1 + 3, "z": 1 + 2 * (6 + 3) + 3}
    per_part = [
        6 + (4 if passed else 1) * ((3 if direct else 4) + 4)
        for _, parts in BATCHES
        for *_, passed, direct in parts
    ]
    return sum(per_group[kind] for kind, _ in GROUPS) + sum(per_part)


def local(partials, worker_residual, server_residual, master, first_moment, second_moment):
    grads = partials.reshape(NY, NH, NX, NL * NC, ROWS, 128)
    wres = worker_residual.reshape(NL * NC, ROWS, 128)
    flat = [v.reshape(ROWS, 128) for v in (server_residual, master, first_moment, second_moment)]
    n = copies_needed()
    hbm = pl.BlockSpec(memory_space=pltpu.HBM)
    vmem = pl.BlockSpec(memory_space=pltpu.VMEM)
    tall = max(r for _, r in GROUPS)
    z_rows = sum(r for kind, r in GROUPS if kind == "z")
    shard = pltpu.VMEM((ROWS, 128), F32)
    results = pl.pallas_call(
        kernel,
        out_shape=(shard, shard, shard, pltpu.VMEM((NY, NH, NX, NL, NC, ROWS, 128), BF)),
        in_specs=[hbm] * 6,
        out_specs=(vmem,) * 4,
        scratch_shapes=[
            pltpu.VMEM((NY, NH, NX, NL * NC, ROWS, 128), BF),
            pltpu.VMEM((NL * NC, ROWS, 128), F32),
            pltpu.VMEM((4, ROWS, 128), F32),
            pltpu.VMEM((2, 6, 4, 2, ROWS, 128), BF),
            pltpu.VMEM((NY, NX, NL * NC, max(z_rows, 16), 128), BF),
            pltpu.VMEM((2, 4, 2, 2, tall, 128), F32),
            pltpu.VMEM((2, 4, 2, 2, ROWS, 128), BF),
            pltpu.VMEM((2, 2, 2, ROWS, 128), F32),
            pltpu.VMEM((2, 3, 2, 2, ROWS, 128), BF),
            pltpu.VMEM((NL * NC, ROWS, 128), BF),
            pltpu.VMEM((NL * NC, ROWS, 128), BF),
            pltpu.VMEM((NL * NC, ROWS, 128), F32),
            pltpu.VMEM((3, ROWS, 128), F32),
            pltpu.SemaphoreType.DMA((len(GROUPS) + 5,)),
            pltpu.SemaphoreType.DMA((n,)),
            pltpu.SemaphoreType.DMA((n,)),
        ],
        compiler_params=pltpu.CompilerParams(collective_id=0, has_side_effects=True, vmem_limit_bytes=44 * 2**20),
    )(*[pltpu.with_memory_space_constraint(v, pltpu.HBM) for v in (grads, wres, *flat)])
    new_mast, new_first, new_second, full = pl.pallas_call(
        write_out,
        out_shape=[jax.ShapeDtypeStruct(v.shape, v.dtype) for v in results],
        in_specs=[pl.BlockSpec(memory_space=pl.ANY)] * 4,
        out_specs=[pl.BlockSpec(memory_space=pl.ANY)] * 4,
        scratch_shapes=[pltpu.SemaphoreType.DMA((3 + NY * NH,))],
        compiler_params=pltpu.CompilerParams(vmem_limit_bytes=2**20),
    )(*[pltpu.with_memory_space_constraint(v, pltpu.VMEM) for v in results])
    return new_mast[None], new_first[None], new_second[None], full.reshape(NY * NH * NX * NL * NC * ROWS, 128)


def solution(mesh):
    placed = (
        P(("outer", "fsdp"), None, None),
        P("outer", "fsdp", None),
        P("fsdp", "outer", None),
        P("fsdp", "outer", None),
        P("fsdp", "outer", None),
        P("fsdp", "outer", None),
    )
    return jax.shard_map(
        local,
        mesh=mesh,
        in_specs=placed,
        out_specs=(P("fsdp", "outer", None), P("fsdp", "outer", None), P("fsdp", "outer", None), P()),
        check_vma=False,
    )
```

```python
import functools

import jax
import jax.numpy as jnp
from jax import lax
from jax.experimental import pallas as pl
from jax.experimental.pallas import tpu as pltpu
from jax.sharding import PartitionSpec as P

STEP = 10
MESH = pl.DeviceIdType.MESH
BF, F32 = jnp.bfloat16, jnp.float32
NX, NY, NH, NL, NC = 4, 4, 2, 2, 2
ROWS = 256

GROUPS = (("n", 48), ("n", 32), ("z", 32), ("z", 32), ("n", 96), ("z", 16))
BATCHES = (
    ((0,), (("yzx", 0, 16, 0, 0),)),
    ((0,), (("yzx", 16, 16, 0, 0),)),
    ((0,), (("yxz", 32, 16, 0, 1),)),
    ((1, 2), (("xzy", 48, 48, 0, 0),)),
    ((1, 2), (("xyz", 96, 16, 0, 0),)),
    ((3,), (("yxz", 112, 16, 0, 0),)),
    ((3,), (("xyz", 128, 16, 0, 0),)),
    ((4,), (("yzx", 144, 48, 0, 0), ("zxy", 192, 32, 0, 0), ("xyz", 224, 16, 1, 0))),
    ((5,), (("xzy", 240, 16, 0, 0),)),
)
LAG = 12
ORDER = (
    ("z1", 2), ("a1", 4), ("a1", 1), ("a2", 4), ("z1", 3), ("a2", 1), ("a1", 0), ("a3", 4),
    ("z2", 2), ("a3", 1), ("z1", 5), ("a2", 0), ("z2", 3), ("a2", 2), ("b", 4), ("z2", 5),
    ("b", 1), ("a3", 0), ("a2", 3), ("a3", 2), ("c", 4), ("a2", 5), ("c", 1), ("a3", 3),
    ("b", 0), ("a3", 5), ("b", 2), ("d", 4), ("d", 1), ("g0", 7), ("b", 3), ("b", 5),
    ("d", 2), ("c", 0), ("g0", 3), ("g0", 4), ("g1", 7), ("d", 3), ("d", 5), ("g0", 5),
    ("g0", 6), ("g0", 8), ("d", 0), ("g1", 3), ("g0", 0), ("g0", 1), ("g0", 2), ("g1", 4),
    ("g1", 5), ("g1", 6), ("g1", 8), ("g2", 7), ("g1", 0), ("g1", 1), ("g1", 2), ("g2", 4),
    ("g2", 3), ("g2", 5), ("g2", 6), ("g2", 8), ("g2", 0), ("g2", 1), ("g3", 4), ("g3", 7),
    ("g3", 5), ("g2", 2), ("g3", 0), ("g3", 6), ("g3", 3), ("g4", 4), ("g3", 1), ("g3", 8),
    ("g4", 5), ("g4", 7), ("g3", 2), ("g4", 0), ("g4", 1), ("g4", 3), ("g4", 6), ("g4", 2),
    ("g4", 8),
)


class At:
    def __init__(self):
        o, f = lax.axis_index("outer"), lax.axis_index("fsdp")
        self.o, self.f = o, f
        self.zl, self.c = o // 2, o % 2
        self.y, self.zh, self.x = f // 8, (f // 4) % 2, f % 4
        self.z = self.zh * 2 + self.zl

    def device(self, x=0, y=0, z=0, c=0):
        z = (self.z + z) % 4
        return {
            "outer": (z % 2) * 2 + (self.c + c) % 2,
            "fsdp": ((self.y + y) % 4) * 8 + (z // 2) * 4 + (self.x + x) % 4,
        }

    def pod(self, j):
        return (self.zl + j // 2) % 2, (self.c + j % 2) % 2


def partners():
    found = {(0, 0, 0, 1)}
    for b in range(1, 4):
        found |= {(b, 0, 0, 0), (0, b, 0, 0), (0, 0, b, 0)}
    return sorted(found)


class Copies:
    def __init__(self, send, recv):
        self.send, self.recv, self.n, self.started = send, recv, 0, []

    def __call__(self, src, dst, to):
        copy = pltpu.make_async_remote_copy(
            src_ref=src, dst_ref=dst, send_sem=self.send.at[self.n], recv_sem=self.recv.at[self.n],
            device_id=to, device_id_type=MESH,
        )
        self.n += 1
        copy.start()
        self.started.append(copy)
        return copy


def kernel(parts_hbm, wres_hbm, sres_hbm, mast_hbm, mom1_hbm, mom2_hbm, new_mast, new_first, new_second, full,
           grads, wres, own, got_a, got_z, sum32, sum16, own32, got_b, out16, got_c, deq, got_o,
           load_sem, send_sem, recv_sem):
    at = At()
    n_groups = len(GROUPS)
    kinds = [kind for kind, _ in GROUPS]
    sizes = [r for _, r in GROUPS]
    rows = [pl.ds(sum(sizes[:g]), r) for g, r in enumerate(sizes)]

    loads = []
    for g in range(n_groups):
        view = (slice(None),) * 4 + (rows[g],)
        loads.append(pltpu.make_async_copy(parts_hbm.at[view], grads.at[view], load_sem.at[g]))
    small = [
        pltpu.make_async_copy(src, dst, load_sem.at[n_groups + i])
        for i, (src, dst) in enumerate(
            [(wres_hbm, wres), (sres_hbm, own.at[0]), (mast_hbm, own.at[1]), (mom1_hbm, own.at[2]), (mom2_hbm, own.at[3])]
        )
    ]
    for copy in loads + small:
        copy.start()

    barrier = pltpu.get_barrier_semaphore()
    met = partners()
    for x, y, z, c in met:
        pl.semaphore_signal(barrier, inc=1, device_id=at.device(x, y, z, c), device_id_type=MESH)
    zl, c = at.pod(3)
    pl.semaphore_signal(barrier, inc=1, device_id={"outer": zl * 2 + c, "fsdp": at.f}, device_id_type=MESH)
    pl.semaphore_wait(barrier, len(met) + 1)

    send = Copies(send_sem, recv_sem)
    mine = (at.x, at.y)
    a, b, c_, d, z = {}, {}, {}, {}, {}

    def chunk(g, s, to, h):
        if kinds[g] == "n":
            return grads.at[:, h, to, 0:2, rows[g], :] if s == 0 else grads.at[to, h, :, 2:4, rows[g], :]
        if s == 0:
            return grads.at[:, at.zh, to, h:h + 1, rows[g], :]
        return grads.at[to, at.zh, :, 2 + h:3 + h, rows[g], :]

    def along(s, n):
        return at.device(x=n) if s == 0 else at.device(y=n)

    def into(g, s, k):
        return got_a.at[s, k, :, 0:(2 if kinds[g] == "n" else 1), rows[g], :]

    def ring(g):
        for s in range(2):
            i = mine[s]
            ahead, behind, across = (i + 1) % 4, (i + 3) % 4, (i + 2) % 4
            a[g, s] = [
                send(chunk(g, s, across, 0), into(g, s, 0), along(s, 1)),
                send(chunk(g, s, across, 1), into(g, s, 1), along(s, 3)),
                send(chunk(g, s, ahead, 1), into(g, s, 2), along(s, 1)),
                send(chunk(g, s, behind, 0), into(g, s, 3), along(s, 3)),
            ]

    def a1(g):
        loads[g].wait()
        ring(g)

    def z_rows(g):
        return pl.ds(sum(r for kind, r in GROUPS[:g] if kind == "z"), sizes[g])

    def z1(g):
        loads[g].wait()
        z[g] = send(grads.at[:, 1 - at.zh, :, :, rows[g], :], got_z.at[:, :, :, z_rows(g), :], at.device(z=2))

    def z2(g):
        z[g].wait_recv()
        for y in range(NY):
            block = grads.at[y, at.zh, :, :, rows[g], :]
            block[...] = (block[...].astype(F32) + got_z[y, :, :, z_rows(g), :].astype(F32)).astype(BF)
        ring(g)

    def a2(g):
        for s in range(2):
            i = mine[s]
            for k, to, n in ((0, (i + 1) % 4, 1), (1, (i + 3) % 4, 3)):
                a[g, s][k].wait_recv()
                block = chunk(g, s, to, k)
                block[...] = (block[...].astype(F32) + into(g, s, k)[...].astype(F32)).astype(BF)
                a[g, s].append(send(block, into(g, s, 4 + k), along(s, n)))

    def a3(g):
        nz = 2 if kinds[g] == "n" else 1
        for s in range(2):
            i, j = mine[s], mine[1 - s]
            for h, (k, m) in enumerate(((4, 3), (2, 5))):
                a[g, s][k].wait_recv()
                a[g, s][m].wait_recv()
                summed = chunk(g, s, i, h)[...].astype(F32) + into(g, s, k)[...].astype(F32) + into(g, s, m)[...].astype(F32)
                if nz == 2:
                    sum32[s, :, h, :, 0:sizes[g], :] = summed
                    sum16[s, :, h, :, rows[g], :] = summed.astype(BF)
                else:
                    sum32[s, :, 0, h:h + 1, 0:sizes[g], :] = summed
                    sum16[s, :, 0, h:h + 1, rows[g], :] = summed.astype(BF)
            b[g, s] = [
                send(sum16.at[s, (j + n) % 4, 0:nz, :, rows[g], :], got_b.at[s, n - 1, 0:nz, :, rows[g], :], along(1 - s, n))
                for n in (1, 3, 2)
            ]
            own32[s, 0:nz, :, rows[g], :] = sum32[s, j, 0:nz, :, 0:sizes[g], :]

    def b1(g):
        for s in range(2):
            for copy in b[g, s]:
                copy.wait_recv()

            def second(h):
                total = own32[s, h, :, rows[g], :]
                for n in range(3):
                    total = total + got_b[s, n, h, :, rows[g], :].astype(F32)
                return total

            both = slice(2 * s, 2 * s + 2)
            if kinds[g] == "n":
                out16[both, rows[g], :] = second(1 - at.zh).astype(BF)
                deq[both, rows[g], :] = second(at.zh)
            else:
                deq[both, rows[g], :] = second(0)
        if kinds[g] == "n":
            c_[g] = send(out16.at[:, rows[g], :], got_c.at[:, rows[g], :], at.device(z=2))
        else:
            code(g, deq[:, rows[g], :])

    def c1(g):
        c_[g].wait_recv()
        code(g, deq[:, rows[g], :] + got_c[:, rows[g], :].astype(F32))

    def code(g, pod_grad):
        worker = pod_grad + wres[:, rows[g], :]
        scale = jnp.max(jnp.abs(worker), axis=-1, keepdims=True) + 1e-06
        coded = (worker / scale).astype(BF)
        deq[:, rows[g], :] = coded.astype(F32) * scale
        d[g] = []
        for j in range(1, 4):
            zl, c = at.pod(j)
            d[g].append(send(deq.at[zl * 2 + c, rows[g], :], got_o.at[j - 1, rows[g], :], {"outer": zl * 2 + c, "fsdp": at.f}))

    def d1(g):
        total = deq[at.o, rows[g], :]
        for j in range(3):
            d[g][j].wait_recv()
            total = total + got_o[j, rows[g], :]
        server = total + own[0, rows[g], :]
        scale = jnp.max(jnp.abs(server), axis=-1, keepdims=True) + 1e-06
        server_code = (server / scale).astype(BF)
        grad = server_code.astype(F32) * scale
        first = 0.9 * own[2, rows[g], :] + 0.1 * grad
        second = 0.95 * own[3, rows[g], :] + 0.05 * grad * grad
        first_hat = first / (1.0 - 0.9**STEP)
        second_hat = second / (1.0 - 0.95**STEP)
        old = own[1, rows[g], :]
        new = old - 0.01 * (first_hat / (jnp.sqrt(second_hat) + 1e-08) + 0.1 * old)
        new_mast[rows[g], :] = new
        new_first[rows[g], :] = first
        new_second[rows[g], :] = second
        full[at.y, at.zh, at.x, at.zl, at.c, rows[g], :] = new.astype(BF)

    def region(part, along_a=None, at_b=None, at_c=0):
        order, first, count = part[:3]
        here = {"x": at.x, "y": at.y, "z": at.z}
        pick = {order[2]: (here[order[2]] + at_c) % 4}
        if at_b is not None:
            pick[order[1]] = (here[order[1]] + at_b) % 4
        if along_a == "own":
            pick[order[0]] = here[order[0]]
        every = slice(None)
        half = order[0] if along_a in (0, 1) else None
        if "z" in pick:
            zh, zl = pick["z"] // 2, pick["z"] % 2
        else:
            zh, zl = (slice(along_a, along_a + 1) if half == "z" else every), every
        for axis in "xy":
            if axis not in pick:
                pick[axis] = slice(2 * along_a, 2 * along_a + 2) if half == axis else every
        return full.at[pick["y"], zh, pick["x"], zl, at.c, pl.ds(first, count), :]

    def to_axis(axis, n):
        return at.device(**{axis: n})

    sibling = at.device(c=1)
    cores, ga, gb, gc, gd = [], {}, {}, {}, {}

    def twin(part, *at_):
        piece = region(part, None, *at_)
        cores.append(send(piece, piece, sibling))

    def third(part, at_b):
        piece = region(part, None, at_b)
        gc[part, at_b] = [send(piece, piece, to_axis(part[0][2], n)) for n in (1, 3)]
        if part[4]:
            gd[part, at_b] = [send(piece, piece, to_axis(part[0][2], 2))]

    def blocks(part):
        return (0, 3, 1, 2) if part[3] else (None,)

    def g0(parts):
        for part in parts:
            piece = region(part, "own", 0)
            ga[part] = [send(piece, piece, to_axis(part[0][0], n)) for n in (1, 3, 2)]

    def g1(parts):
        for part in parts:
            for copy in ga[part]:
                copy.wait_recv()
            piece = region(part, None, 0)
            gb[part] = [send(piece, piece, to_axis(part[0][1], n)) for n in (1, 3, 2)]
            if part[3]:
                third(part, 0)

    def g2(parts):
        for i, at_b in enumerate((3, 1, 2)):
            for part in parts:
                gb[part][i].wait_recv()
                if part[3]:
                    third(part, at_b)
                elif i == 2:
                    third(part, None)
        for part in parts:
            for at_b in blocks(part):
                twin(part, at_b)

    def g3(parts):
        for i in range(4):
            for part in parts:
                if i >= len(blocks(part)):
                    continue
                at_b, axis = blocks(part)[i], part[0][2]
                for copy in gc[part, at_b]:
                    copy.wait_recv()
                if not part[4]:
                    back, front = region(part, 0, at_b, 3), region(part, 1, at_b, 1)
                    gd[part, at_b] = [send(back, back, to_axis(axis, 1)), send(front, front, to_axis(axis, 3))]
                twin(part, at_b, 1)
                twin(part, at_b, 3)

    def g4(parts):
        for i in range(4):
            for part in parts:
                if i >= len(blocks(part)):
                    continue
                at_b = blocks(part)[i]
                for copy in gd[part, at_b]:
                    copy.wait_recv()
                twin(part, at_b, 2)

    steps = {"a1": a1, "a2": a2, "a3": a3, "z1": z1, "z2": z2, "b": b1, "c": c1, "d": d1}
    gathers = {"g0": g0, "g1": g1, "g2": g2, "g3": g3, "g4": g4}
    for copy in small:
        copy.wait()
    ended, n_cores = [], []
    for i, (name, n) in enumerate(ORDER):
        if name in steps:
            steps[name](n)
        else:
            gathers[name](BATCHES[n][1])
        ended.append(len(send.started))
        n_cores.append(len(cores))
        if i >= LAG:
            for copy in send.started[ended[i - LAG - 1] if i > LAG else 0:ended[i - LAG]]:
                copy.wait_send()
            for copy in cores[n_cores[i - LAG - 1] if i > LAG else 0:n_cores[i - LAG]]:
                copy.wait_recv()
    for copy in cores[n_cores[-LAG - 1]:]:
        copy.wait_recv()
    for copy in send.started[ended[-LAG - 1]:]:
        copy.wait_send()


def write_out(*refs):
    n = len(refs) // 2
    sem = refs[-1]
    pairs = [(refs[i], refs[n + i]) for i in range(n - 1)]
    pairs += [(refs[n - 1].at[y, h], refs[2 * n - 1].at[y, h]) for y in range(NY) for h in range(NH)]
    copies = [pltpu.make_async_copy(src, dst, sem.at[i]) for i, (src, dst) in enumerate(pairs)]
    for copy in copies:
        copy.start()
    for copy in copies:
        copy.wait()


def copies_needed():
    per_group = {"n": 2 * (6 + 3) + 1 + 3, "z": 1 + 2 * (6 + 3) + 3}
    per_part = [
        6 + (4 if passed else 1) * ((3 if direct else 4) + 4)
        for _, parts in BATCHES
        for *_, passed, direct in parts
    ]
    return sum(per_group[kind] for kind, _ in GROUPS) + sum(per_part)


def local(partials, worker_residual, server_residual, master, first_moment, second_moment):
    grads = partials.reshape(NY, NH, NX, NL * NC, ROWS, 128)
    wres = worker_residual.reshape(NL * NC, ROWS, 128)
    flat = [v.reshape(ROWS, 128) for v in (server_residual, master, first_moment, second_moment)]
    n = copies_needed()
    hbm = pl.BlockSpec(memory_space=pltpu.HBM)
    vmem = pl.BlockSpec(memory_space=pltpu.VMEM)
    tall = max(r for _, r in GROUPS)
    z_rows = sum(r for kind, r in GROUPS if kind == "z")
    shard = pltpu.VMEM((ROWS, 128), F32)
    results = pl.pallas_call(
        kernel,
        out_shape=(shard, shard, shard, pltpu.VMEM((NY, NH, NX, NL, NC, ROWS, 128), BF)),
        in_specs=[hbm] * 6,
        out_specs=(vmem,) * 4,
        scratch_shapes=[
            pltpu.VMEM((NY, NH, NX, NL * NC, ROWS, 128), BF),
            pltpu.VMEM((NL * NC, ROWS, 128), F32),
            pltpu.VMEM((4, ROWS, 128), F32),
            pltpu.VMEM((2, 6, 4, 2, ROWS, 128), BF),
            pltpu.VMEM((NY, NX, NL * NC, max(z_rows, 16), 128), BF),
            pltpu.VMEM((2, 4, 2, 2, tall, 128), F32),
            pltpu.VMEM((2, 4, 2, 2, ROWS, 128), BF),
            pltpu.VMEM((2, 2, 2, ROWS, 128), F32),
            pltpu.VMEM((2, 3, 2, 2, ROWS, 128), BF),
            pltpu.VMEM((NL * NC, ROWS, 128), BF),
            pltpu.VMEM((NL * NC, ROWS, 128), BF),
            pltpu.VMEM((NL * NC, ROWS, 128), F32),
            pltpu.VMEM((3, ROWS, 128), F32),
            pltpu.SemaphoreType.DMA((len(GROUPS) + 5,)),
            pltpu.SemaphoreType.DMA((n,)),
            pltpu.SemaphoreType.DMA((n,)),
        ],
        compiler_params=pltpu.CompilerParams(collective_id=0, has_side_effects=True, vmem_limit_bytes=44 * 2**20),
    )(*[pltpu.with_memory_space_constraint(v, pltpu.HBM) for v in (grads, wres, *flat)])
    new_mast, new_first, new_second, full = pl.pallas_call(
        write_out,
        out_shape=[jax.ShapeDtypeStruct(v.shape, v.dtype) for v in results],
        in_specs=[pl.BlockSpec(memory_space=pl.ANY)] * 4,
        out_specs=[pl.BlockSpec(memory_space=pl.ANY)] * 4,
        scratch_shapes=[pltpu.SemaphoreType.DMA((3 + NY * NH,))],
        compiler_params=pltpu.CompilerParams(vmem_limit_bytes=2**20),
    )(*[pltpu.with_memory_space_constraint(v, pltpu.VMEM) for v in results])
    return new_mast[None], new_first[None], new_second[None], full.reshape(NY * NH * NX * NL * NC * ROWS, 128)


def solution(mesh):
    placed = (
        P(("outer", "fsdp"), None, None),
        P("outer", "fsdp", None),
        P("fsdp", "outer", None),
        P("fsdp", "outer", None),
        P("fsdp", "outer", None),
        P("fsdp", "outer", None),
    )
    return jax.shard_map(
        local,
        mesh=mesh,
        in_specs=placed,
        out_specs=(P("fsdp", "outer", None), P("fsdp", "outer", None), P("fsdp", "outer", None), P()),
        check_vma=False,
    )
```
